256 devices in a mesh: dp: 4 (over y), mp: 64 (over z, x, core).
Axes of the slice: x: 4, y: 4, z: 8, core: 2. Of those that a mesh axis runs over, the one named last changes fastest.
Arguments:
- queries: bfloat16 [3, 2048, 4096], P(None, 'dp', 'mp'), may hold values from -15 to 15
- memory: bfloat16 [1024, 4096], P('mp'), may hold values from -6 to 6
- w_key: bfloat16 [3, 4096, 4096], P(None, 'mp'), may hold values from -0.09375 to 0.09375
- w_value: bfloat16 [3, 4096, 4096], P(None, 'mp'), may hold values from -0.09375 to 0.09375
- grad_out: bfloat16 [3, 2048, 4096], P(None, 'dp', 'mp'), may hold values from -6 to 6
Outputs:
- attended: bfloat16 [3, 2048, 4096], P(None, 'dp', 'mp')
- grad_queries: bfloat16 [3, 2048, 4096], P(None, 'dp', 'mp')
- grad_memory: float32 [1024, 4096], P('mp')
- grad_w_key: float32 [3, 4096, 4096], P(None, 'mp')
- grad_w_value: float32 [3, 4096, 4096], P(None, 'mp')
The draws below stay inside these ranges and needn't reach their ends.
All inputs are finite; a program needn't handle non-finite values.
Results may differ from the reference program's by a relative error of at most 0.025.
Values may be sent and summed in bfloat16 or wider, within the bound.
No kernel may reach another device: no remote copies, remote signals or barrier semaphores. Data moves between devices by JAX's collectives and lax.ppermute only.
A program may use at most 128 MiB of HBM per device.

```python
import jax
import jax.numpy as jnp
from jax import lax

D = 4096
HEAD_COUNT = 64
HEAD_WIDTH = 64
LAYERS = 3
E = 4096
ENCODER_TOKENS = 1024
DECODER_TOKENS = 2048


def draw_queries(key, part):
    key = jax.random.fold_in(key, 7)
    base = jax.random.truncated_normal(key, -4.0, 4.0, (LAYERS, DECODER_TOKENS, HEAD_COUNT * HEAD_WIDTH), jnp.float32) * 0.375
    return base.astype(jnp.bfloat16)


def level_of(own_key, shape, shards, smallest, largest):
    factor_of, own = 1.0, jax.random.fold_in(own_key, 6)
    for axis_at, blocks in shards:
        steps = jnp.exp(jax.random.uniform(jax.random.fold_in(own, axis_at), (blocks,), jnp.float32, smallest / len(shards), largest / len(shards)))
        factor_of = factor_of * jnp.repeat(steps, shape[axis_at] // blocks).reshape([-1 if axis == axis_at else 1 for axis in range(len(shape))])
    return factor_of


def noise(stream_key, extent, width, limit, cuts=(), held_as=jnp.bfloat16):
    result = jax.random.normal(stream_key, extent, jnp.float32) * width
    if len(cuts) > 0:
        result = level_of(stream_key, extent, cuts, -0.22, 0.18) * result
    return jnp.clip(result, min=-limit, max=limit).astype(held_as)


def setup_inputs(seed: int = 0) -> dict:
    key_of = jax.random.split(jax.random.key(seed), 6)
    return {
        "queries": draw_queries(jax.random.fold_in(key_of[5], 71), 0),
        "memory": noise(key_of[1], (ENCODER_TOKENS, D), 1.0, 6.0, ((0, 64),)),
        "w_key": noise(key_of[2], (LAYERS, E, D), D ** -0.5, 0.09375, ((1, 64),)),
        "w_value": noise(key_of[3], (LAYERS, E, D), D ** -0.5, 0.09375, ((1, 64),)),
        "grad_out": noise(key_of[4], (LAYERS, DECODER_TOKENS, E), 1.0, 6.0, ((1, 4), (2, 64))),
    }


def reference(queries, memory, w_key, w_value, grad_out):
    attended = []
    grad_queries = []
    grad_w_key = []
    grad_w_value = []
    grad_memory = jnp.zeros((ENCODER_TOKENS, memory.shape[1]), jnp.float32)
    for layer in range(LAYERS):
        keys = jnp.dot(memory, w_key[layer].T, preferred_element_type=jnp.float32).astype(jnp.bfloat16)
        values = jnp.dot(memory, w_value[layer].T, preferred_element_type=jnp.float32).astype(jnp.bfloat16)
        per_head_queries = queries[layer].reshape(DECODER_TOKENS, HEAD_COUNT, HEAD_WIDTH).astype(jnp.float32)
        per_head_keys = keys.reshape(ENCODER_TOKENS, HEAD_COUNT, HEAD_WIDTH).astype(jnp.float32)
        per_head_values = values.reshape(ENCODER_TOKENS, HEAD_COUNT, HEAD_WIDTH).astype(jnp.float32)
        head_output_gradient = grad_out[layer].reshape(DECODER_TOKENS, HEAD_COUNT, HEAD_WIDTH).astype(jnp.float32)
        attention_logits = jnp.einsum('fke,pke->kfp', per_head_queries, per_head_keys)
        row_max = jnp.max(attention_logits, axis=-1, keepdims=True)
        exp_scores = jnp.exp(attention_logits - row_max)
        attn_probs = exp_scores / jnp.sum(exp_scores, axis=-1, keepdims=True)
        batch_probabilities = lax.optimization_barrier(attn_probs.astype(jnp.bfloat16)).astype(jnp.float32)
        attended_output = jnp.einsum('kqc,cke->qke', batch_probabilities, per_head_values).reshape(DECODER_TOKENS, HEAD_COUNT * HEAD_WIDTH)
        attended.append(attended_output.astype(jnp.bfloat16))
        probability_gradient = jnp.einsum('fke,pke->kfp', head_output_gradient, per_head_values)
        row_delta = jnp.sum(attn_probs * probability_gradient, axis=-1, keepdims=True)
        logit_gradient = lax.optimization_barrier((attn_probs * (probability_gradient - row_delta)).astype(jnp.bfloat16)).astype(jnp.float32)
        query_gradient = jnp.einsum('kqc,cke->qke', logit_gradient, per_head_keys).reshape(DECODER_TOKENS, HEAD_COUNT * HEAD_WIDTH)
        grad_queries.append(query_gradient.astype(jnp.bfloat16))
        key_gradient = jnp.einsum('vlk,lvu->kvu', logit_gradient, per_head_queries).reshape(ENCODER_TOKENS, HEAD_COUNT * HEAD_WIDTH).astype(jnp.bfloat16)
        value_gradient = jnp.einsum('vlk,lvu->kvu', batch_probabilities, head_output_gradient).reshape(ENCODER_TOKENS, HEAD_COUNT * HEAD_WIDTH).astype(jnp.bfloat16)
        grad_w_key.append(jnp.dot(key_gradient.T, memory, preferred_element_type=jnp.float32))
        grad_w_value.append(jnp.dot(value_gradient.T, memory, preferred_element_type=jnp.float32))
        grad_memory = grad_memory + jnp.dot(key_gradient, w_key[layer], preferred_element_type=jnp.float32)
        grad_memory = grad_memory + jnp.dot(value_gradient, w_value[layer], preferred_element_type=jnp.float32)
    return (jnp.stack(attended), jnp.stack(grad_queries), grad_memory, jnp.stack(grad_w_key), jnp.stack(grad_w_value))
```

```python
import jax
import jax.numpy as jnp
from jax import lax
from jax.experimental import pallas as pl
from jax.experimental.pallas import tpu as pltpu
from jax.sharding import Mesh
from jax.sharding import PartitionSpec as P

HEAD_WIDTH = 64
BF16 = jnp.bfloat16
F32 = jnp.float32
NT = (((1,), (1,)), ((), ()))
TN = (((0,), (0,)), ((), ()))
SWAP = [(0, 1), (1, 0)]


def mm(a, b, dims=(((1,), (0,)), ((), ()))):
    return lax.dot_general(a, b, dims, preferred_element_type=F32)


def split_heads(own_ref, other_ref, layer):
    lanes = slice(layer * 2 * HEAD_WIDTH, (layer + 1) * 2 * HEAD_WIDTH)
    both = jnp.concatenate([own_ref[:, lanes], other_ref[:, lanes]], axis=0).astype(F32)
    left = lax.broadcasted_iota(jnp.int32, both.shape, 1) < HEAD_WIDTH
    keys = jnp.where(left, both, 0.0).astype(BF16)
    values = jnp.where(left, 0.0, both).astype(BF16)
    return keys, values


def stats_kernel(own_ref, other_ref, qdo_ref, stats_ref):
    parts, layers, rows, _ = qdo_ref.shape
    stats_ref[...] = jnp.zeros_like(stats_ref)
    for layer in range(layers):
        keys, values = split_heads(own_ref, other_ref, layer)
        for part in range(parts):
            q = qdo_ref[part, layer]
            scores = mm(keys, q, NT)
            grads = mm(values, q, NT)
            top = jnp.max(scores, axis=0, keepdims=True)
            e = jnp.exp(scores - top)
            total = jnp.sum(e, axis=0, keepdims=True)
            delta = jnp.sum(e * grads, axis=0, keepdims=True) / total
            at = slice(part * rows, (part + 1) * rows)
            stats_ref[layer : layer + 1, at] = top + jnp.log(total)
            stats_ref[layers + layer : layers + layer + 1, at] = delta


def grads_kernel(own_ref, other_ref, qdo_ref, s0, s1, s2, s3, g_ref, qa_ref):
    parts, layers, rows, width = qdo_ref.shape
    tokens = 2 * own_ref.shape[0]
    left = lax.broadcasted_iota(jnp.int32, (tokens, width), 1) < HEAD_WIDTH
    stats = [s[...] for s in (s0, s1, s2, s3)]
    lses = [s[0:layers] for s in stats]
    top = jnp.maximum(jnp.maximum(lses[0], lses[1]), jnp.maximum(lses[2], lses[3]))
    total = sum(jnp.exp(a - top) for a in lses)
    lse = top + jnp.log(total)
    delta = sum(jnp.exp(s[0:layers] - lse) * s[layers : 2 * layers] for s in stats)
    for layer in range(layers):
        keys, values = split_heads(own_ref, other_ref, layer)
        flipped = jnp.concatenate([keys, values], axis=0).astype(F32).T.astype(BF16)
        acc = jnp.zeros((2 * tokens, width), F32)
        for part in range(parts):
            at = slice(part * rows, (part + 1) * rows)
            q = qdo_ref[part, layer]
            scores = mm(keys, q, NT)
            grads = mm(values, q, NT)
            probs = jnp.exp(scores - lse[layer : layer + 1, at])
            dscores = (probs * (grads - delta[layer : layer + 1, at])).astype(BF16)
            both = jnp.concatenate([dscores, probs.astype(BF16)], axis=0)
            acc += mm(both, q)
            qa_ref[part, layer] = mm(flipped, both).T.astype(BF16)
        g_ref[:, layer * width : (layer + 1) * width] = jnp.where(left, acc[:tokens], acc[tokens:]).astype(BF16)


def weights_kernel(g_ref, own_ref, other_ref, key_ref, value_ref):
    half = own_ref.shape[0]
    layers, width, _ = key_ref.shape
    out = mm(g_ref[:, :half], own_ref[...]) + mm(g_ref[:, half:], other_ref[...])
    for layer in range(layers):
        at = 2 * layer * width
        key_ref[layer] = out[at : at + width]
        value_ref[layer] = out[at + width : at + 2 * width]


def cost(flops, moved, exps=0):
    return pl.CostEstimate(flops=flops, bytes_accessed=moved, transcendentals=exps)


def shards(queries, memory, w_key, w_value, grad_out):
    layers, rows, width = queries.shape
    dp, nz, nx = lax.axis_size("dp"), lax.axis_size("z"), lax.axis_size("x")
    mine, d = memory.shape
    few = mine // dp
    here = lax.axis_index("dp")
    cols = 2 * width * layers
    half = few * nz * nx
    params = pltpu.CompilerParams(vmem_limit_bytes=48 * 1024 * 1024)

    full_own = lax.all_gather(memory, ("z", "x"), axis=0, tiled=True)
    full_other = lax.ppermute(full_own, "core", SWAP)

    quarter = lax.dynamic_slice(memory, (here * few, 0), (few, d))
    along_z = lax.all_to_all(jnp.broadcast_to(quarter, (nz, few, d)), "z", 0, 0).reshape(nz * few, d)
    mem_own = lax.all_to_all(jnp.broadcast_to(along_z, (nx, nz * few, d)), "x", 0, 0).reshape(half, d)
    mem_other = lax.ppermute(mem_own, "core", SWAP)

    qdo_own = jnp.concatenate([queries, grad_out], axis=-1)
    qdo = lax.all_to_all(jnp.broadcast_to(qdo_own, (dp,) + qdo_own.shape), "dp", 0, 0)

    w = jnp.concatenate([w_key, w_value], axis=1).reshape(cols, d)
    kv_own = mm(mem_own, w, NT).astype(BF16)
    kv_other = mm(mem_other, w, NT).astype(BF16)

    all_rows = dp * rows
    work = layers * all_rows * 2 * half * 256
    stats = pl.pallas_call(
        stats_kernel,
        out_shape=jax.ShapeDtypeStruct((8, all_rows), F32),
        compiler_params=params,
        cost_estimate=cost(4 * work, 4 * qdo.size, layers * all_rows * 2 * half),
    )(kv_own, kv_other, qdo)
    others = [lax.ppermute(stats, "dp", [(a, (a + s) % dp) for a in range(dp)]) for s in range(1, dp)]
    g, qa = pl.pallas_call(
        grads_kernel,
        out_shape=(
            jax.ShapeDtypeStruct((2 * half, cols), BF16),
            jax.ShapeDtypeStruct(qdo.shape, BF16),
        ),
        compiler_params=params,
        cost_estimate=cost(12 * work, 8 * qdo.size, layers * all_rows * 2 * half),
    )(kv_own, kv_other, qdo, stats, *others)

    to_other = mm(g[half:], w).astype(BF16)
    from_other = lax.ppermute(to_other, "core", SWAP)
    part = (mm(g[:half], w) + from_other.astype(F32)).astype(BF16)
    part = lax.all_to_all(part.reshape(nx, nz * few, d), "x", 0, 0)
    part = jnp.sum(part.astype(F32), axis=0).astype(BF16)
    part = lax.all_to_all(part.reshape(nz, few, d), "z", 0, 0)
    part = jnp.sum(part.astype(F32), axis=0)
    grad_memory = lax.all_to_all(jnp.broadcast_to(part, (dp, few, d)), "dp", 0, 0).reshape(mine, d)

    qa = lax.all_to_all(qa, "dp", 0, 0)
    qa = jnp.sum(qa.astype(F32), axis=0).astype(BF16)
    grad_queries, attended = qa[..., :width], qa[..., width:]

    g_all = lax.all_to_all(jnp.broadcast_to(g, (dp,) + g.shape), "dp", 0, 0)
    g_all = g_all.reshape(dp, 2, nx, nz, few, cols).transpose(5, 1, 3, 2, 0, 4).reshape(cols, 2 * nz * nx * mine)
    block = 512
    gw_shape = jax.ShapeDtypeStruct((layers, width, d), F32)
    gw_spec = pl.BlockSpec((layers, width, block), lambda n: (0, 0, n))
    mem_spec = pl.BlockSpec((nz * nx * mine, block), lambda n: (0, n))
    grad_w_key, grad_w_value = pl.pallas_call(
        weights_kernel,
        grid=(d // block,),
        in_specs=[pl.BlockSpec(g_all.shape, lambda n: (0, 0)), mem_spec, mem_spec],
        out_specs=(gw_spec, gw_spec),
        out_shape=(gw_shape, gw_shape),
        compiler_params=params,
        cost_estimate=cost(2 * cols * 2 * nz * nx * mine * d, 4 * nz * nx * mine * d + 4 * cols * d),
    )(g_all, full_own, full_other)
    return (attended, grad_queries, grad_memory, grad_w_key, grad_w_value)


def solution(mesh):
    dp = mesh.shape["dp"]
    split = Mesh(mesh.devices.reshape(dp, -1, 4, 2), ("dp", "z", "x", "core"))
    mp = ("z", "x", "core")
    by_rows, by_heads = P(None, "dp", mp), P(None, mp, None)
    return jax.shard_map(
        shards,
        mesh=split,
        in_specs=(by_rows, P(mp, None), by_heads, by_heads, by_rows),
        out_specs=(by_rows, by_rows, P(mp, None), by_heads, by_heads),
        check_vma=False,
    )
```

```python
import jax
import jax.numpy as jnp
from jax import lax
from jax.experimental import pallas as pl
from jax.experimental.pallas import tpu as pltpu
from jax.sharding import Mesh
from jax.sharding import PartitionSpec as P

HEAD_WIDTH = 64
BF16 = jnp.bfloat16
F32 = jnp.float32
NT = (((1,), (1,)), ((), ()))


def mm(a, b, dims=(((1,), (0,)), ((), ()))):
    return lax.dot_general(a, b, dims, preferred_element_type=F32)


def shift(x, axis, by):
    n = lax.axis_size(axis)
    return lax.ppermute(x, axis, [(a, (a + by) % n) for a in range(n)])


def after(x, *others):
    return lax.optimization_barrier((x, *others))[0]


def split_heads(own_ref, other_ref, layer):
    lanes = slice(layer * 2 * HEAD_WIDTH, (layer + 1) * 2 * HEAD_WIDTH)
    both = jnp.concatenate([own_ref[:, lanes], other_ref[:, lanes]], axis=0).astype(F32)
    left = lax.broadcasted_iota(jnp.int32, both.shape, 1) < HEAD_WIDTH
    keys = jnp.where(left, both, 0.0).astype(BF16)
    values = jnp.where(left, 0.0, both).astype(BF16)
    return keys, values


def project_kernel(own_key, own_value, other_key, other_value, *refs):
    *mem_refs, own_ref, other_ref = refs
    mem = jnp.concatenate([m[...] for m in mem_refs], axis=0)
    layers, width, _ = own_key.shape
    for key, value, out_ref in ((other_key, other_value, other_ref), (own_key, own_value, own_ref)):
        for layer in range(layers):
            w = jnp.concatenate([key[layer], value[layer]], axis=0)
            at = 2 * layer * width
            out_ref[:, at : at + 2 * width] = mm(w, mem, NT).T.astype(BF16)


def memory_kernel(own_ref, other_ref, own_key, own_value, other_key, other_value, out_ref):
    layers, width, d = own_key.shape
    blocks, rows, _ = out_ref.shape
    g = jnp.concatenate([own_ref[: blocks * rows], other_ref[...]], axis=1)
    step = 512
    for at in range(0, d, step):
        w = [r[layer, :, at : at + step] for k, v in ((own_key, own_value), (other_key, other_value)) for layer in range(layers) for r in (k, v)]
        out = mm(g, jnp.concatenate(w, axis=0)).astype(BF16)
        out_ref[:, :, at : at + step] = out.reshape(blocks, rows, step)


def stats_kernel(own_ref, other_ref, *refs):
    *qdo_refs, stats_ref = refs
    layers, _, rows = qdo_refs[0].shape
    stats_ref[...] = jnp.zeros_like(stats_ref)
    for layer in range(layers):
        keys, values = split_heads(own_ref, other_ref, layer)
        for part, qdo_ref in enumerate(qdo_refs):
            q = qdo_ref[layer]
            scores = mm(keys, q)
            grads = mm(values, q)
            top = jnp.max(scores, axis=0, keepdims=True)
            e = jnp.exp(scores - top)
            total = jnp.sum(e, axis=0, keepdims=True)
            delta = jnp.sum(e * grads, axis=0, keepdims=True) / total
            at = slice(part * rows, (part + 1) * rows)
            stats_ref[layer : layer + 1, at] = top + jnp.log(total)
            stats_ref[layers + layer : layers + layer + 1, at] = delta


def combine(stats_refs, rows, layers):
    parts = len(stats_refs)
    for part in range(parts):
        stats = []
        for k, s in enumerate(stats_refs):
            at = (part - k) % parts * rows
            stats.append(s[:, at : at + rows])
        lses = [s[0:layers] for s in stats]
        top = jnp.maximum(jnp.maximum(lses[0], lses[1]), jnp.maximum(lses[2], lses[3]))
        lse = top + jnp.log(sum(jnp.exp(a - top) for a in lses))
        yield lse, sum(jnp.exp(s[0:layers] - lse) * s[layers : 2 * layers] for s in stats)


def probs_and_scores(keys, values, q, lse, delta):
    probs = jnp.exp(mm(keys, q) - lse)
    dscores = probs * (mm(values, q) - delta)
    return jnp.concatenate([dscores.astype(BF16), probs.astype(BF16)], axis=0)


def token_grads_kernel(own_ref, other_ref, *refs):
    *qdo_refs, s0, s1, s2, s3, g_ref = refs
    layers, width, rows = qdo_refs[0].shape
    tokens = 2 * own_ref.shape[0]
    left = lax.broadcasted_iota(jnp.int32, (tokens, width), 1) < HEAD_WIDTH
    stats = list(combine((s0, s1, s2, s3), rows, layers))
    for layer in range(layers):
        keys, values = split_heads(own_ref, other_ref, layer)
        acc = 0.0
        for qdo_ref, (lse, delta) in zip(qdo_refs, stats):
            q = qdo_ref[layer]
            acc += mm(probs_and_scores(keys, values, q, lse[layer : layer + 1], delta[layer : layer + 1]), q, NT)
        g_ref[:, layer * width : (layer + 1) * width] = jnp.where(left, acc[:tokens], acc[tokens:]).astype(BF16)


def row_grads_kernel(own_ref, other_ref, *refs):
    *qdo_refs, s0, s1, s2, s3, qa_ref = refs
    layers, _, rows = qdo_refs[0].shape
    stats = list(combine((s0, s1, s2, s3), rows, layers))
    for layer in range(layers):
        keys, values = split_heads(own_ref, other_ref, layer)
        flipped = jnp.concatenate([keys, values], axis=0).astype(F32).T.astype(BF16)
        for part, (qdo_ref, (lse, delta)) in enumerate(zip(qdo_refs, stats)):
            both = probs_and_scores(keys, values, qdo_ref[layer], lse[layer : layer + 1], delta[layer : layer + 1])
            qa_ref[part, layer] = mm(flipped, both).astype(BF16)


def weights_kernel(at_ref, *refs):
    *g_refs, mem_ref, key_ref, value_ref, stack, order, flipped = refs
    ndp, nx, nz, few = len(g_refs), 4, 8, 4
    layers, width, _ = key_ref.shape

    @pl.when(pl.program_id(0) == 0)
    def _():
        for part, g_ref in enumerate(g_refs):
            stack[part] = g_ref[...].astype(F32)
        parts = [lax.rem(at_ref[0] + ndp - dp, ndp) for dp in range(ndp)]
        for half in range(2):
            core = at_ref[2] if half == 0 else 1 - at_ref[2]
            for back in range(nx):
                x = lax.rem(at_ref[1] + nx - back, nx)
                first = (half * nx + back) * nz * few
                blocks = [stack[part, first : first + nz * few] for part in parts]
                for z in range(nz):
                    to = pl.multiple_of(((z * nx + x) * 2 + core) * ndp * few, ndp * few)
                    order[pl.ds(to, ndp * few)] = jnp.concatenate([b[z * few : (z + 1) * few] for b in blocks], axis=0)
        flipped[...] = order[...].T.astype(BF16)

    out = mm(flipped[...], mem_ref[...])
    for layer in range(layers):
        at = 2 * layer * width
        key_ref[layer] = out[at : at + width]
        value_ref[layer] = out[at + width : at + 2 * width]


def cost(flops, moved, exps=0):
    return pl.CostEstimate(flops=flops, bytes_accessed=moved, transcendentals=exps)


def shards(queries, memory, w_key, w_value, grad_out):
    layers, rows, width = queries.shape
    dp, nz, nx = lax.axis_size("dp"), lax.axis_size("z"), lax.axis_size("x")
    mine, d = memory.shape
    few = mine // dp
    here = lax.axis_index("dp")
    cols = 2 * width * layers
    half = few * nz * nx
    params = pltpu.CompilerParams(vmem_limit_bytes=28 * 1024 * 1024)

    at = jnp.stack([here, lax.axis_index("x"), lax.axis_index("core")])

    full = lax.all_gather(memory, ("z", "x", "core"), axis=0, tiled=True)

    quarter = lax.dynamic_slice(memory, (here * few, 0), (few, d))
    along_z = lax.all_to_all(jnp.broadcast_to(quarter, (nz, few, d)), "z", 0, 0).reshape(nz * few, d)
    key_other, value_other = shift(w_key, "core", 1), shift(w_value, "core", 1)
    along_z, key_other, value_other = lax.optimization_barrier((along_z, key_other, value_other))
    qdo = jnp.concatenate([queries.swapaxes(1, 2), grad_out.swapaxes(1, 2)], axis=1)
    qdo = after(qdo, along_z)
    qdo = [qdo] + [shift(qdo, "dp", s) for s in range(1, dp)]

    mem_parts = [along_z] + [shift(along_z, "x", s) for s in range(1, nx)]

    weights = (w_key, w_value, key_other, value_other)
    kv_own, kv_other = pl.pallas_call(
        project_kernel,
        out_shape=(jax.ShapeDtypeStruct((half, cols), BF16), jax.ShapeDtypeStruct((half, cols), BF16)),
        compiler_params=params,
        cost_estimate=cost(4 * half * cols * d, 2 * (half + 2 * cols) * d),
    )(*weights, *mem_parts)
    kv_other = shift(kv_other, "core", 1)

    all_rows = dp * rows
    work = layers * all_rows * 2 * half * 256
    stats = pl.pallas_call(
        stats_kernel,
        out_shape=jax.ShapeDtypeStruct((8, all_rows), F32),
        compiler_params=params,
        cost_estimate=cost(4 * work, 4 * dp * qdo[0].size, layers * all_rows * 2 * half),
    )(kv_own, kv_other, *qdo)
    others = [shift(stats, "dp", s) for s in range(1, dp)]
    g = pl.pallas_call(
        token_grads_kernel,
        out_shape=jax.ShapeDtypeStruct((2 * half, cols), BF16),
        compiler_params=params,
        cost_estimate=cost(8 * work, 4 * dp * qdo[0].size, layers * all_rows * 2 * half),
    )(kv_own, kv_other, *qdo, stats, *others)

    g_other = shift(g[half:], "core", 1)
    part = pl.pallas_call(
        memory_kernel,
        out_shape=jax.ShapeDtypeStruct((nx, nz * few, d), BF16),
        compiler_params=params,
        cost_estimate=cost(4 * half * cols * d, 2 * (half + 2 * cols) * d),
    )(g, g_other, *weights)
    g_all = [g] + [shift(g, "dp", s) for s in range(1, dp)]
    stats = after(stats, part, g_all[1], g_all[3])
    part = sum([part[0].astype(F32)] + [shift(part[s], "x", -s).astype(F32) for s in range(1, nx)]).astype(BF16)

    qa = pl.pallas_call(
        row_grads_kernel,
        out_shape=jax.ShapeDtypeStruct((dp,) + qdo[0].shape, BF16),
        compiler_params=params,
        cost_estimate=cost(8 * work, 8 * dp * qdo[0].size, layers * all_rows * 2 * half),
    )(kv_own, kv_other, *qdo, stats, *others)
    qa = [qa[0]] + [shift(qa[s], "dp", -s) for s in range(1, dp)]

    block = 512
    gw_shape = jax.ShapeDtypeStruct((layers, width, d), F32)
    gw_spec = pl.BlockSpec((layers, width, block), lambda n, at: (0, 0, n))
    grad_w = pl.pallas_call(
        weights_kernel,
        grid_spec=pltpu.PrefetchScalarGridSpec(
            num_scalar_prefetch=1,
            grid=(d // block,),
            in_specs=[pl.BlockSpec(g.shape, lambda n, at: (0, 0))] * dp + [pl.BlockSpec((full.shape[0], block), lambda n, at: (0, n))],
            out_specs=(gw_spec, gw_spec),
            scratch_shapes=[pltpu.VMEM((dp,) + g.shape, F32), pltpu.VMEM((full.shape[0], cols), F32), pltpu.VMEM((cols, full.shape[0]), BF16)],
        ),
        out_shape=(gw_shape, gw_shape),
        compiler_params=pltpu.CompilerParams(vmem_limit_bytes=56 * 1024 * 1024),
        cost_estimate=cost(2 * cols * full.size, 2 * full.size + 4 * cols * d),
    )(at, *g_all, full)

    part = lax.all_to_all(part.reshape(nz, few, d), "z", 0, 0)
    part = jnp.sum(part.astype(F32), axis=0)
    part, grad_w_key, grad_w_value = lax.optimization_barrier((part, *grad_w))
    parts = [part] + [shift(part, "dp", s) for s in range(1, dp)]
    parts = jnp.concatenate([parts[-1 - j % dp] for j in range(2 * dp - 1)], axis=0)
    grad_memory = lax.dynamic_slice(parts, ((dp - 1 - here) * few, 0), (mine, d))
    qa = sum(a.astype(F32) for a in qa).astype(BF16)
    grad_queries, attended = qa[:, :width].swapaxes(1, 2), qa[:, width:].swapaxes(1, 2)
    return (attended, grad_queries, grad_memory, grad_w_key, grad_w_value)


def solution(mesh):
    dp = mesh.shape["dp"]
    split = Mesh(mesh.devices.reshape(dp, -1, 4, 2), ("dp", "z", "x", "core"))
    mp = ("z", "x", "core")
    by_rows, by_heads = P(None, "dp", mp), P(None, mp, None)
    return jax.shard_map(
        shards,
        mesh=split,
        in_specs=(by_rows, P(mp, None), by_heads, by_heads, by_rows),
        out_specs=(by_rows, by_rows, P(mp, None), by_heads, by_heads),
        check_vma=False,
    )
```

```python
import jax
import jax.numpy as jnp
from jax import lax
from jax.experimental import pallas as pl
from jax.experimental.pallas import tpu as pltpu
from jax.sharding import Mesh
from jax.sharding import PartitionSpec as P

HEAD_WIDTH = 64
BF16 = jnp.bfloat16
F32 = jnp.float32
NT = (((1,), (1,)), ((), ()))


def mm(a, b, dims=(((1,), (0,)), ((), ()))):
    return lax.dot_general(a, b, dims, preferred_element_type=F32)


def shift(x, axis, by):
    n = lax.axis_size(axis)
    return lax.ppermute(x, axis, [(a, (a + by) % n) for a in range(n)])


def after(x, *others):
    return lax.optimization_barrier((x, *others))[0]


def split_heads(own_ref, other_ref, layer):
    lanes = slice(layer * 2 * HEAD_WIDTH, (layer + 1) * 2 * HEAD_WIDTH)
    both = jnp.concatenate([own_ref[:, lanes], other_ref[:, lanes]], axis=0).astype(F32)
    left = lax.broadcasted_iota(jnp.int32, both.shape, 1) < HEAD_WIDTH
    keys = jnp.where(left, both, 0.0).astype(BF16)
    values = jnp.where(left, 0.0, both).astype(BF16)
    return keys, values


def project_kernel(own_key, own_value, other_key, other_value, *refs):
    *mem_refs, own_ref, other_ref = refs
    mem = jnp.concatenate([m[...] for m in mem_refs], axis=0)
    layers, width, _ = own_key.shape
    for key, value, out_ref in ((other_key, other_value, other_ref), (own_key, own_value, own_ref)):
        for layer in range(layers):
            w = jnp.concatenate([key[layer], value[layer]], axis=0)
            at = 2 * layer * width
            out_ref[:, at : at + 2 * width] = mm(w, mem, NT).T.astype(BF16)


def memory_kernel(own_ref, other_ref, own_key, own_value, other_key, other_value, *out_refs):
    layers, width, d = own_key.shape
    blocks, rows = len(out_refs), out_refs[0].shape[0]
    g = jnp.concatenate([own_ref[: blocks * rows], other_ref[...]], axis=1)
    step = 512
    for at in range(0, d, step):
        w = [r[layer, :, at : at + step] for k, v in ((own_key, own_value), (other_key, other_value)) for layer in range(layers) for r in (k, v)]
        out = mm(g, jnp.concatenate(w, axis=0)).astype(BF16)
        for x, out_ref in enumerate(out_refs):
            out_ref[:, at : at + step] = out[x * rows : (x + 1) * rows]


def stats_kernel(own_ref, other_ref, *refs):
    *qdo_refs, stats_ref = refs
    layers, _, rows = qdo_refs[0].shape
    stats_ref[...] = jnp.zeros_like(stats_ref)
    for layer in range(layers):
        keys, values = split_heads(own_ref, other_ref, layer)
        for part, qdo_ref in enumerate(qdo_refs):
            q = qdo_ref[layer]
            scores = mm(keys, q)
            grads = mm(values, q)
            top = jnp.max(scores, axis=0, keepdims=True)
            e = jnp.exp(scores - top)
            total = jnp.sum(e, axis=0, keepdims=True)
            delta = jnp.sum(e * grads, axis=0, keepdims=True) / total
            at = slice(part * rows, (part + 1) * rows)
            stats_ref[layer : layer + 1, at] = top + jnp.log(total)
            stats_ref[layers + layer : layers + layer + 1, at] = delta


def combine(stats_refs, rows, layers):
    parts = len(stats_refs)
    for part in range(parts):
        stats = []
        for k, s in enumerate(stats_refs):
            at = (part - k) % parts * rows
            stats.append(s[:, at : at + rows])
        lses = [s[0:layers] for s in stats]
        top = jnp.maximum(jnp.maximum(lses[0], lses[1]), jnp.maximum(lses[2], lses[3]))
        lse = top + jnp.log(sum(jnp.exp(a - top) for a in lses))
        yield lse, sum(jnp.exp(s[0:layers] - lse) * s[layers : 2 * layers] for s in stats)


def probs_and_scores(keys, values, q, lse, delta):
    probs = jnp.exp(mm(keys, q) - lse)
    dscores = probs * (mm(values, q) - delta)
    return jnp.concatenate([dscores.astype(BF16), probs.astype(BF16)], axis=0)


def grads_kernel(own_ref, other_ref, *refs):
    n = len(refs) // 3
    qdo_refs, stats_refs, g_ref, qa_refs = refs[:n], refs[n : 2 * n], refs[2 * n], refs[2 * n + 1 :]
    layers, width, rows = qdo_refs[0].shape
    tokens = 2 * own_ref.shape[0]
    left = lax.broadcasted_iota(jnp.int32, (tokens, width), 1) < HEAD_WIDTH
    stats = list(combine(stats_refs, rows, layers))
    for layer in range(layers):
        keys, values = split_heads(own_ref, other_ref, layer)
        flipped = jnp.concatenate([keys, values], axis=0).astype(F32).T.astype(BF16)
        acc = 0.0
        for part, (qdo_ref, (lse, delta)) in enumerate(zip(qdo_refs, stats)):
            q = qdo_ref[layer]
            both = probs_and_scores(keys, values, q, lse[layer : layer + 1], delta[layer : layer + 1])
            acc += mm(both, q, NT)
            qa_refs[part][layer] = mm(flipped, both).astype(BF16)
        g_ref[:, layer * width : (layer + 1) * width] = jnp.where(left, acc[:tokens], acc[tokens:]).astype(BF16)


def order_kernel(at_ref, *refs):
    *g_refs, out_ref, stack, order = refs
    ndp, nx, nz, few = 2 * len(g_refs), 4, 8, 4
    for pair, g_ref in enumerate(g_refs):
        for part in range(2):
            stack[2 * pair + part] = g_ref[part].astype(F32)
    parts = [lax.bitwise_xor(at_ref[0], dp) for dp in range(ndp)]
    for half in range(2):
        core = at_ref[2] if half == 0 else 1 - at_ref[2]
        for back in range(nx):
            x = lax.rem(at_ref[1] + nx - back, nx)
            first = (half * nx + back) * nz * few
            blocks = [stack[part, first : first + nz * few] for part in parts]
            for z in range(nz):
                to = pl.multiple_of(((z * nx + x) * 2 + core) * ndp * few, ndp * few)
                order[pl.ds(to, ndp * few)] = jnp.concatenate([b[z * few : (z + 1) * few] for b in blocks], axis=0)
    out_ref[...] = order[...].T.astype(BF16)


def weights_kernel(g_ref, mem_ref, key_ref, value_ref):
    layers, width, _ = key_ref.shape
    out = mm(g_ref[...], mem_ref[...])
    for layer in range(layers):
        at = 2 * layer * width
        key_ref[layer] = out[at : at + width]
        value_ref[layer] = out[at + width : at + 2 * width]


def cost(flops, moved, exps=0):
    return pl.CostEstimate(flops=flops, bytes_accessed=moved, transcendentals=exps)


def shards(queries, memory, w_key, w_value, grad_out):
    layers, rows, width = queries.shape
    dp, nz, nx = lax.axis_size("dp"), lax.axis_size("z"), lax.axis_size("x")
    mine, d = memory.shape
    few = mine // dp
    here = lax.axis_index("dp")
    cols = 2 * width * layers
    half = few * nz * nx
    params = pltpu.CompilerParams(vmem_limit_bytes=28 * 1024 * 1024)

    at = jnp.stack([here, lax.axis_index("x"), lax.axis_index("core")])

    full = lax.all_gather(memory, ("z", "x", "core"), axis=0, tiled=True)

    quarter = lax.dynamic_slice(memory, (here * few, 0), (few, d))
    along_z = lax.all_to_all(jnp.broadcast_to(quarter, (nz, few, d)), "z", 0, 0).reshape(nz * few, d)
    key_other, value_other = shift(w_key, "core", 1), shift(w_value, "core", 1)
    along_z, key_other, value_other = lax.optimization_barrier((along_z, key_other, value_other))
    qdo = jnp.concatenate([queries.swapaxes(1, 2), grad_out.swapaxes(1, 2)], axis=1)
    qdo = after(qdo, along_z)
    qdo = [qdo] + [shift(qdo, "dp", s) for s in range(1, dp)]

    mem_parts = [along_z] + [shift(along_z, "x", s) for s in range(1, nx)]

    weights = (w_key, w_value, key_other, value_other)
    kv_own, kv_other = pl.pallas_call(
        project_kernel,
        out_shape=(jax.ShapeDtypeStruct((half, cols), BF16), jax.ShapeDtypeStruct((half, cols), BF16)),
        compiler_params=params,
        cost_estimate=cost(4 * half * cols * d, 2 * (half + 2 * cols) * d),
    )(*weights, *mem_parts)
    kv_other = shift(kv_other, "core", 1)

    all_rows = dp * rows
    work = layers * all_rows * 2 * half * 256
    stats = pl.pallas_call(
        stats_kernel,
        out_shape=jax.ShapeDtypeStruct((8, all_rows), F32),
        compiler_params=params,
        cost_estimate=cost(4 * work, 4 * dp * qdo[0].size, layers * all_rows * 2 * half),
    )(kv_own, kv_other, *qdo)
    others = [shift(stats, "dp", s) for s in range(1, dp)]
    g, *qa = pl.pallas_call(
        grads_kernel,
        out_shape=[jax.ShapeDtypeStruct((2 * half, cols), BF16)] + [jax.ShapeDtypeStruct(qdo[0].shape, BF16)] * dp,
        compiler_params=params,
        cost_estimate=cost(12 * work, 8 * dp * qdo[0].size, layers * all_rows * 2 * half),
    )(kv_own, kv_other, *qdo, stats, *others)

    g_other = shift(g[half:], "core", 1)
    part = pl.pallas_call(
        memory_kernel,
        out_shape=[jax.ShapeDtypeStruct((nz * few, d), BF16)] * nx,
        compiler_params=params,
        cost_estimate=cost(4 * half * cols * d, 2 * (half + 2 * cols) * d),
    )(g, g_other, *weights)
    g_all = jnp.stack([g, lax.ppermute(g, "dp", [(a, a ^ 1) for a in range(dp)])])
    g_all = (g_all, lax.ppermute(g_all, "dp", [(a, a ^ 2) for a in range(dp)]))
    part = sum([part[0].astype(F32)] + [shift(part[s], "x", -s).astype(F32) for s in range(1, nx)]).astype(BF16)

    flipped = pl.pallas_call(
        order_kernel,
        in_specs=[pl.BlockSpec(memory_space=pltpu.SMEM)] + [pl.BlockSpec(memory_space=pltpu.VMEM)] * 2,
        out_shape=jax.ShapeDtypeStruct((cols, full.shape[0]), BF16),
        scratch_shapes=[pltpu.VMEM((dp,) + g.shape, F32), pltpu.VMEM((full.shape[0], cols), F32)],
        compiler_params=params,
        cost_estimate=cost(0, 8 * cols * full.shape[0]),
    )(at, *g_all)
    block = 1024
    gw_shape = jax.ShapeDtypeStruct((layers, width, d), F32)
    gw_spec = pl.BlockSpec((layers, width, block), lambda n: (0, 0, n))
    grad_w = pl.pallas_call(
        weights_kernel,
        grid=(d // block,),
        in_specs=[pl.BlockSpec(flipped.shape, lambda n: (0, 0)), pl.BlockSpec((full.shape[0], block), lambda n: (0, n))],
        out_specs=(gw_spec, gw_spec),
        out_shape=(gw_shape, gw_shape),
        compiler_params=pltpu.CompilerParams(vmem_limit_bytes=56 * 1024 * 1024),
        cost_estimate=cost(2 * cols * full.size, 2 * full.size + 4 * cols * d),
    )(flipped, full)

    qa[1], qa[3] = shift(qa[1], "dp", -1), shift(qa[3], "dp", -3)
    part, *qa = lax.optimization_barrier((part, *qa))
    qa[2] = shift(qa[2], "dp", -2)

    part = lax.all_to_all(part.reshape(nz, few, d), "z", 0, 0)
    part, grad_w_key, grad_w_value = lax.optimization_barrier((part, *grad_w))
    part = jnp.sum(part.astype(F32), axis=0)
    parts = [part] + [shift(part, "dp", s) for s in range(1, dp)]
    parts = jnp.concatenate([parts[-1 - j % dp] for j in range(2 * dp - 1)], axis=0)
    grad_memory = lax.dynamic_slice(parts, ((dp - 1 - here) * few, 0), (mine, d))
    part, *qa = lax.optimization_barrier((part, *qa))
    qa = sum(a.astype(F32) for a in qa).astype(BF16)
    grad_queries, attended = qa[:, :width].swapaxes(1, 2), qa[:, width:].swapaxes(1, 2)
    return (attended, grad_queries, grad_memory, grad_w_key, grad_w_value)


def solution(mesh):
    dp = mesh.shape["dp"]
    split = Mesh(mesh.devices.reshape(dp, -1, 4, 2), ("dp", "z", "x", "core"))
    mp = ("z", "x", "core")
    by_rows, by_heads = P(None, "dp", mp), P(None, mp, None)
    return jax.shard_map(
        shards,
        mesh=split,
        in_specs=(by_rows, P(mp, None), by_heads, by_heads, by_rows),
        out_specs=(by_rows, by_rows, P(mp, None), by_heads, by_heads),
        check_vma=False,
    )
```

```python
import jax
import jax.numpy as jnp
from jax import lax
from jax.experimental import pallas as pl
from jax.experimental.pallas import tpu as pltpu
from jax.sharding import Mesh
from jax.sharding import PartitionSpec as P

HEAD_WIDTH = 64
BF16 = jnp.bfloat16
F32 = jnp.float32
NT = (((1,), (1,)), ((), ()))


def mm(a, b, dims=(((1,), (0,)), ((), ()))):
    return lax.dot_general(a, b, dims, preferred_element_type=F32)


def shift(x, axis, by):
    n = lax.axis_size(axis)
    return lax.ppermute(x, axis, [(a, (a + by) % n) for a in range(n)])


def after(x, *others):
    return lax.optimization_barrier((x, *others))[0]


def split_heads(own_ref, other_ref, layer):
    lanes = slice(layer * 2 * HEAD_WIDTH, (layer + 1) * 2 * HEAD_WIDTH)
    both = jnp.concatenate([own_ref[:, lanes], other_ref[:, lanes]], axis=0).astype(F32)
    left = lax.broadcasted_iota(jnp.int32, both.shape, 1) < HEAD_WIDTH
    keys = jnp.where(left, both, 0.0).astype(BF16)
    values = jnp.where(left, 0.0, both).astype(BF16)
    return keys, values


def project_kernel(own_key, own_value, other_key, other_value, *refs):
    *mem_refs, own_ref, other_ref = refs
    mem = jnp.concatenate([m[...] for m in mem_refs], axis=0)
    layers, width, _ = own_key.shape
    for key, value, out_ref in ((other_key, other_value, other_ref), (own_key, own_value, own_ref)):
        for layer in range(layers):
            w = jnp.concatenate([key[layer], value[layer]], axis=0)
            at = 2 * layer * width
            out_ref[:, at : at + 2 * width] = mm(w, mem, NT).T.astype(BF16)


def memory_kernel(own_ref, other_ref, own_key, own_value, other_key, other_value, *out_refs):
    layers, width, d = own_key.shape
    blocks, rows = len(out_refs), out_refs[0].shape[0]
    g = jnp.concatenate([own_ref[: blocks * rows], other_ref[...]], axis=1)
    step = 512
    for at in range(0, d, step):
        w = [r[layer, :, at : at + step] for k, v in ((own_key, own_value), (other_key, other_value)) for layer in range(layers) for r in (k, v)]
        out = mm(g, jnp.concatenate(w, axis=0)).astype(BF16)
        for x, out_ref in enumerate(out_refs):
            out_ref[:, at : at + step] = out[x * rows : (x + 1) * rows]


def stats_kernel(own_ref, other_ref, *refs):
    *qdo_refs, stats_ref = refs
    layers, _, rows = qdo_refs[0].shape
    stats_ref[...] = jnp.zeros_like(stats_ref)
    for layer in range(layers):
        keys, values = split_heads(own_ref, other_ref, layer)
        for part, qdo_ref in enumerate(qdo_refs):
            q = qdo_ref[layer]
            scores = mm(keys, q)
            grads = mm(values, q)
            top = jnp.max(scores, axis=0, keepdims=True)
            e = jnp.exp(scores - top)
            total = jnp.sum(e, axis=0, keepdims=True)
            delta = jnp.sum(e * grads, axis=0, keepdims=True) / total
            at = slice(part * rows, (part + 1) * rows)
            stats_ref[layer : layer + 1, at] = top + jnp.log(total)
            stats_ref[layers + layer : layers + layer + 1, at] = delta


def combine(stats_refs, rows, layers):
    parts = len(stats_refs)
    for part in range(parts):
        stats = []
        for k, s in enumerate(stats_refs):
            at = (part - k) % parts * rows
            stats.append(s[:, at : at + rows])
        lses = [s[0:layers] for s in stats]
        top = jnp.maximum(jnp.maximum(lses[0], lses[1]), jnp.maximum(lses[2], lses[3]))
        lse = top + jnp.log(sum(jnp.exp(a - top) for a in lses))
        yield lse, sum(jnp.exp(s[0:layers] - lse) * s[layers : 2 * layers] for s in stats)


def probs_and_scores(keys, values, q, lse, delta):
    probs = jnp.exp(mm(keys, q) - lse)
    dscores = probs * (mm(values, q) - delta)
    return jnp.concatenate([dscores.astype(BF16), probs.astype(BF16)], axis=0)


def grads_kernel(own_ref, other_ref, *refs):
    n = len(refs) // 3
    qdo_refs, stats_refs, g_ref, qa_refs = refs[:n], refs[n : 2 * n], refs[2 * n], refs[2 * n + 1 :]
    layers, width, rows = qdo_refs[0].shape
    tokens = 2 * own_ref.shape[0]
    left = lax.broadcasted_iota(jnp.int32, (tokens, width), 1) < HEAD_WIDTH
    stats = list(combine(stats_refs, rows, layers))
    for layer in range(layers):
        keys, values = split_heads(own_ref, other_ref, layer)
        flipped = jnp.concatenate([keys, values], axis=0).astype(F32).T.astype(BF16)
        acc = 0.0
        for part, (qdo_ref, (lse, delta)) in enumerate(zip(qdo_refs, stats)):
            q = qdo_ref[layer]
            both = probs_and_scores(keys, values, q, lse[layer : layer + 1], delta[layer : layer + 1])
            acc += mm(both, q, NT)
            qa_refs[part][layer] = mm(flipped, both).astype(BF16)
        g_ref[:, layer * width : (layer + 1) * width] = jnp.where(left, acc[:tokens], acc[tokens:]).astype(BF16)


def weights_kernel(at_ref, *refs):
    *g_refs, mem_ref, key_ref, value_ref, stack, order, flipped = refs
    ndp, nx, nz, few = 2 * len(g_refs), 4, 8, 4
    layers, width, _ = key_ref.shape

    @pl.when(pl.program_id(0) == 0)
    def _():
        for pair, g_ref in enumerate(g_refs):
            for part in range(2):
                stack[2 * pair + part] = g_ref[part].astype(F32)
        parts = [lax.bitwise_xor(at_ref[0], dp) for dp in range(ndp)]
        for half in range(2):
            core = at_ref[2] if half == 0 else 1 - at_ref[2]
            for back in range(nx):
                x = lax.rem(at_ref[1] + nx - back, nx)
                first = (half * nx + back) * nz * few
                blocks = [stack[part, first : first + nz * few] for part in parts]
                for z in range(nz):
                    to = pl.multiple_of(((z * nx + x) * 2 + core) * ndp * few, ndp * few)
                    order[pl.ds(to, ndp * few)] = jnp.concatenate([b[z * few : (z + 1) * few] for b in blocks], axis=0)
        flipped[...] = order[...].T.astype(BF16)

    out = mm(flipped[...], mem_ref[...])
    for layer in range(layers):
        at = 2 * layer * width
        key_ref[layer] = out[at : at + width]
        value_ref[layer] = out[at + width : at + 2 * width]


def cost(flops, moved, exps=0):
    return pl.CostEstimate(flops=flops, bytes_accessed=moved, transcendentals=exps)


def shards(queries, memory, w_key, w_value, grad_out):
    layers, rows, width = queries.shape
    dp, nz, nx = lax.axis_size("dp"), lax.axis_size("z"), lax.axis_size("x")
    mine, d = memory.shape
    few = mine // dp
    here = lax.axis_index("dp")
    cols = 2 * width * layers
    half = few * nz * nx
    params = pltpu.CompilerParams(vmem_limit_bytes=28 * 1024 * 1024)

    at = jnp.stack([here, lax.axis_index("x"), lax.axis_index("core")])

    full = lax.all_gather(memory, ("z", "x", "core"), axis=0, tiled=True)

    quarter = lax.dynamic_slice(memory, (here * few, 0), (few, d))
    along_z = lax.all_to_all(jnp.broadcast_to(quarter, (nz, few, d)), "z", 0, 0).reshape(nz * few, d)
    key_other, value_other = shift(w_key, "core", 1), shift(w_value, "core", 1)
    along_z, key_other, value_other, at = lax.optimization_barrier((along_z, key_other, value_other, at))
    qdo = jnp.concatenate([queries.swapaxes(1, 2), grad_out.swapaxes(1, 2)], axis=1)
    qdo = after(qdo, along_z)
    qdo = [qdo] + [shift(qdo, "dp", s) for s in range(1, dp)]

    mem_parts = [along_z] + [shift(along_z, "x", s) for s in range(1, nx)]

    weights = (w_key, w_value, key_other, value_other)
    kv_own, kv_other = pl.pallas_call(
        project_kernel,
        out_shape=(jax.ShapeDtypeStruct((half, cols), BF16), jax.ShapeDtypeStruct((half, cols), BF16)),
        compiler_params=params,
        cost_estimate=cost(4 * half * cols * d, 2 * (half + 2 * cols) * d),
    )(*weights, *mem_parts)
    kv_other = shift(kv_other, "core", 1)

    all_rows = dp * rows
    work = layers * all_rows * 2 * half * 256
    stats = pl.pallas_call(
        stats_kernel,
        out_shape=jax.ShapeDtypeStruct((8, all_rows), F32),
        compiler_params=params,
        cost_estimate=cost(4 * work, 4 * dp * qdo[0].size, layers * all_rows * 2 * half),
    )(kv_own, kv_other, *qdo)
    others = [shift(stats, "dp", s) for s in range(1, dp)]
    g, *qa = pl.pallas_call(
        grads_kernel,
        out_shape=[jax.ShapeDtypeStruct((2 * half, cols), BF16)] + [jax.ShapeDtypeStruct(qdo[0].shape, BF16)] * dp,
        compiler_params=params,
        cost_estimate=cost(12 * work, 8 * dp * qdo[0].size, layers * all_rows * 2 * half),
    )(kv_own, kv_other, *qdo, stats, *others)

    g_other = shift(g[half:], "core", 1)
    part = pl.pallas_call(
        memory_kernel,
        out_shape=[jax.ShapeDtypeStruct((nz * few, d), BF16)] * nx,
        compiler_params=params,
        cost_estimate=cost(4 * half * cols * d, 2 * (half + 2 * cols) * d),
    )(g, g_other, *weights)
    g_all = jnp.stack([g, lax.ppermute(g, "dp", [(a, a ^ 1) for a in range(dp)])])
    g_all = (g_all, lax.ppermute(g_all, "dp", [(a, a ^ 2) for a in range(dp)]))
    part = sum([part[0].astype(F32)] + [shift(part[s], "x", -s).astype(F32) for s in range(1, nx)]).astype(BF16)

    block = 1024
    gw_shape = jax.ShapeDtypeStruct((layers, width, d), F32)
    gw_spec = pl.BlockSpec((layers, width, block), lambda n, at: (0, 0, n))
    grad_w = pl.pallas_call(
        weights_kernel,
        grid_spec=pltpu.PrefetchScalarGridSpec(
            num_scalar_prefetch=1,
            grid=(d // block,),
            in_specs=[pl.BlockSpec((2,) + g.shape, lambda n, at: (0, 0, 0))] * 2 + [pl.BlockSpec((full.shape[0], block), lambda n, at: (0, n))],
            out_specs=(gw_spec, gw_spec),
            scratch_shapes=[pltpu.VMEM((dp,) + g.shape, F32), pltpu.VMEM((full.shape[0], cols), F32), pltpu.VMEM((cols, full.shape[0]), BF16)],
        ),
        out_shape=(gw_shape, gw_shape),
        compiler_params=pltpu.CompilerParams(vmem_limit_bytes=56 * 1024 * 1024),
        cost_estimate=cost(2 * cols * full.size, 2 * full.size + 4 * cols * d),
    )(at, *g_all, full)

    qa[1] = shift(qa[1], "dp", -1)
    part, qa[2], qa[3] = lax.optimization_barrier((part, qa[2], qa[3]))
    qa[1], qa[2], qa[3] = lax.optimization_barrier((qa[1], qa[2], qa[3]))
    qa[2], qa[3] = shift(qa[2], "dp", -2), shift(qa[3], "dp", -3)

    part = lax.all_to_all(part.reshape(nz, few, d), "z", 0, 0)
    part, grad_w_key, grad_w_value = lax.optimization_barrier((part, *grad_w))
    part = jnp.sum(part.astype(F32), axis=0).astype(BF16)
    parts = [part] + [shift(part, "dp", s) for s in range(1, dp)]
    parts = jnp.concatenate([parts[-1 - j % dp] for j in range(2 * dp - 1)], axis=0)
    grad_memory = lax.dynamic_slice(parts, ((dp - 1 - here) * few, 0), (mine, d)).astype(F32)
    part, *qa = lax.optimization_barrier((part, *qa))
    qa = sum(a.astype(F32) for a in qa).astype(BF16)
    grad_queries, attended = qa[:, :width].swapaxes(1, 2), qa[:, width:].swapaxes(1, 2)
    return (attended, grad_queries, grad_memory, grad_w_key, grad_w_value)


def solution(mesh):
    dp = mesh.shape["dp"]
    split = Mesh(mesh.devices.reshape(dp, -1, 4, 2), ("dp", "z", "x", "core"))
    mp = ("z", "x", "core")
    by_rows, by_heads = P(None, "dp", mp), P(None, mp, None)
    return jax.shard_map(
        shards,
        mesh=split,
        in_specs=(by_rows, P(mp, None), by_heads, by_heads, by_rows),
        out_specs=(by_rows, by_rows, P(mp, None), by_heads, by_heads),
        check_vma=False,
    )
```

```python
import jax
import jax.numpy as jnp
from jax import lax
from jax.experimental import pallas as pl
from jax.experimental.pallas import tpu as pltpu
from jax.sharding import Mesh
from jax.sharding import PartitionSpec as P

HEAD_WIDTH = 64
BF16 = jnp.bfloat16
F32 = jnp.float32
NT = (((1,), (1,)), ((), ()))


def mm(a, b, dims=(((1,), (0,)), ((), ()))):
    return lax.dot_general(a, b, dims, preferred_element_type=F32)


def shift(x, axis, by):
    n = lax.axis_size(axis)
    return lax.ppermute(x, axis, [(a, (a + by) % n) for a in range(n)])


def after(x, *others):
    return lax.optimization_barrier((x, *others))[0]


def split_heads(own_ref, other_ref, layer):
    lanes = slice(layer * 2 * HEAD_WIDTH, (layer + 1) * 2 * HEAD_WIDTH)
    both = jnp.concatenate([own_ref[:, lanes], other_ref[:, lanes]], axis=0).astype(F32)
    left = lax.broadcasted_iota(jnp.int32, both.shape, 1) < HEAD_WIDTH
    keys = jnp.where(left, both, 0.0).astype(BF16)
    values = jnp.where(left, 0.0, both).astype(BF16)
    return keys, values


def project_kernel(own_key, own_value, other_key, other_value, *refs):
    *mem_refs, own_ref, other_ref = refs
    mem = jnp.concatenate([m[...] for m in mem_refs], axis=0)
    layers, width, _ = own_key.shape
    for key, value, out_ref in ((other_key, other_value, other_ref), (own_key, own_value, own_ref)):
        for layer in range(layers):
            w = jnp.concatenate([key[layer], value[layer]], axis=0)
            at = 2 * layer * width
            out_ref[:, at : at + 2 * width] = mm(w, mem, NT).T.astype(BF16)


def memory_kernel(own_ref, other_ref, own_key, own_value, other_key, other_value, *out_refs):
    layers, width, d = own_key.shape
    blocks, rows = len(out_refs), out_refs[0].shape[0]
    g = jnp.concatenate([own_ref[: blocks * rows], other_ref[...]], axis=1)
    step = 512
    for at in range(0, d, step):
        w = [r[layer, :, at : at + step] for k, v in ((own_key, own_value), (other_key, other_value)) for layer in range(layers) for r in (k, v)]
        out = mm(g, jnp.concatenate(w, axis=0)).astype(BF16)
        for x, out_ref in enumerate(out_refs):
            out_ref[:, at : at + step] = out[x * rows : (x + 1) * rows]


def stats_kernel(own_ref, other_ref, *refs):
    *qdo_refs, stats_ref = refs
    layers, _, rows = qdo_refs[0].shape
    stats_ref[...] = jnp.zeros_like(stats_ref)
    for layer in range(layers):
        keys, values = split_heads(own_ref, other_ref, layer)
        for part, qdo_ref in enumerate(qdo_refs):
            q = qdo_ref[layer]
            scores = mm(keys, q)
            grads = mm(values, q)
            top = jnp.max(scores, axis=0, keepdims=True)
            e = jnp.exp(scores - top)
            total = jnp.sum(e, axis=0, keepdims=True)
            delta = jnp.sum(e * grads, axis=0, keepdims=True) / total
            at = slice(part * rows, (part + 1) * rows)
            stats_ref[layer : layer + 1, at] = top + jnp.log(total)
            stats_ref[layers + layer : layers + layer + 1, at] = delta


def combine(stats_refs, rows, layers):
    parts = len(stats_refs)
    for part in range(parts):
        stats = []
        for k, s in enumerate(stats_refs):
            at = (part - k) % parts * rows
            stats.append(s[:, at : at + rows])
        lses = [s[0:layers] for s in stats]
        top = jnp.maximum(jnp.maximum(lses[0], lses[1]), jnp.maximum(lses[2], lses[3]))
        lse = top + jnp.log(sum(jnp.exp(a - top) for a in lses))
        yield lse, sum(jnp.exp(s[0:layers] - lse) * s[layers : 2 * layers] for s in stats)


def probs_and_scores(keys, values, q, lse, delta):
    probs = jnp.exp(mm(keys, q) - lse)
    dscores = probs * (mm(values, q) - delta)
    return jnp.concatenate([dscores.astype(BF16), probs.astype(BF16)], axis=0)


def grads_kernel(own_ref, other_ref, *refs):
    n = len(refs) // 3
    qdo_refs, stats_refs, g_ref, qa_refs = refs[:n], refs[n : 2 * n], refs[2 * n], refs[2 * n + 1 :]
    layers, width, rows = qdo_refs[0].shape
    tokens = 2 * own_ref.shape[0]
    left = lax.broadcasted_iota(jnp.int32, (tokens, width), 1) < HEAD_WIDTH
    stats = list(combine(stats_refs, rows, layers))
    for layer in range(layers):
        keys, values = split_heads(own_ref, other_ref, layer)
        flipped = jnp.concatenate([keys, values], axis=0).astype(F32).T.astype(BF16)
        acc = 0.0
        for part, (qdo_ref, (lse, delta)) in enumerate(zip(qdo_refs, stats)):
            q = qdo_ref[layer]
            both = probs_and_scores(keys, values, q, lse[layer : layer + 1], delta[layer : layer + 1])
            acc += mm(both, q, NT)
            qa_refs[part][layer] = mm(flipped, both).astype(BF16)
        g_ref[:, layer * width : (layer + 1) * width] = jnp.where(left, acc[:tokens], acc[tokens:]).astype(BF16)


def weights_kernel(at_ref, *refs):
    *g_refs, mem_ref, key_ref, value_ref, stack, order, flipped = refs
    ndp, nx, nz, few = 2 * len(g_refs), 4, 8, 4
    layers, width, _ = key_ref.shape

    @pl.when(pl.program_id(0) == 0)
    def _():
        for pair, g_ref in enumerate(g_refs):
            for part in range(2):
                stack[2 * pair + part] = g_ref[part].astype(F32)
        parts = [lax.bitwise_xor(at_ref[0], dp) for dp in range(ndp)]
        for half in range(2):
            core = at_ref[2] if half == 0 else 1 - at_ref[2]
            for back in range(nx):
                x = lax.rem(at_ref[1] + nx - back, nx)
                first = (half * nx + back) * nz * few
                blocks = [stack[part, first : first + nz * few] for part in parts]
                for z in range(nz):
                    to = pl.multiple_of(((z * nx + x) * 2 + core) * ndp * few, ndp * few)
                    order[pl.ds(to, ndp * few)] = jnp.concatenate([b[z * few : (z + 1) * few] for b in blocks], axis=0)
        flipped[...] = order[...].T.astype(BF16)

    out = mm(flipped[...], mem_ref[...])
    for layer in range(layers):
        at = 2 * layer * width
        key_ref[layer] = out[at : at + width]
        value_ref[layer] = out[at + width : at + 2 * width]


def cost(flops, moved, exps=0):
    return pl.CostEstimate(flops=flops, bytes_accessed=moved, transcendentals=exps)


def shards(queries, memory, w_key, w_value, grad_out):
    layers, rows, width = queries.shape
    dp, nz, nx = lax.axis_size("dp"), lax.axis_size("z"), lax.axis_size("x")
    mine, d = memory.shape
    few = mine // dp
    here = lax.axis_index("dp")
    cols = 2 * width * layers
    half = few * nz * nx
    params = pltpu.CompilerParams(vmem_limit_bytes=28 * 1024 * 1024)

    at = jnp.stack([here, lax.axis_index("x"), lax.axis_index("core")])

    full = lax.all_gather(memory, ("z", "x", "core"), axis=0, tiled=True)

    quarter = lax.dynamic_slice(memory, (here * few, 0), (few, d))
    along_z = lax.all_to_all(jnp.broadcast_to(quarter, (nz, few, d)), "z", 0, 0).reshape(nz * few, d)
    key_other, value_other = shift(w_key, "core", 1), shift(w_value, "core", 1)
    along_z, key_other, value_other, at = lax.optimization_barrier((along_z, key_other, value_other, at))
    qdo = jnp.concatenate([queries.swapaxes(1, 2), grad_out.swapaxes(1, 2)], axis=1)
    qdo = after(qdo, along_z)
    qdo = [qdo] + [shift(qdo, "dp", s) for s in range(1, dp)]

    mem_parts = [along_z] + [shift(along_z, "x", s) for s in range(1, nx)]

    weights = (w_key, w_value, key_other, value_other)
    kv_own, kv_other = pl.pallas_call(
        project_kernel,
        out_shape=(jax.ShapeDtypeStruct((half, cols), BF16), jax.ShapeDtypeStruct((half, cols), BF16)),
        compiler_params=params,
        cost_estimate=cost(4 * half * cols * d, 2 * (half + 2 * cols) * d),
    )(*weights, *mem_parts)
    kv_other = shift(kv_other, "core", 1)

    all_rows = dp * rows
    work = layers * all_rows * 2 * half * 256
    stats = pl.pallas_call(
        stats_kernel,
        out_shape=jax.ShapeDtypeStruct((8, all_rows), F32),
        compiler_params=params,
        cost_estimate=cost(4 * work, 4 * dp * qdo[0].size, layers * all_rows * 2 * half),
    )(kv_own, kv_other, *qdo)
    others = [shift(stats, "dp", s) for s in range(1, dp)]
    g, *qa = pl.pallas_call(
        grads_kernel,
        out_shape=[jax.ShapeDtypeStruct((2 * half, cols), BF16)] + [jax.ShapeDtypeStruct(qdo[0].shape, BF16)] * dp,
        compiler_params=params,
        cost_estimate=cost(12 * work, 8 * dp * qdo[0].size, layers * all_rows * 2 * half),
    )(kv_own, kv_other, *qdo, stats, *others)

    g_other = shift(g[half:], "core", 1)
    part = pl.pallas_call(
        memory_kernel,
        out_shape=[jax.ShapeDtypeStruct((nz * few, d), BF16)] * nx,
        compiler_params=params,
        cost_estimate=cost(4 * half * cols * d, 2 * (half + 2 * cols) * d),
    )(g, g_other, *weights)
    g_all = jnp.stack([g, lax.ppermute(g, "dp", [(a, a ^ 1) for a in range(dp)])])
    g_all = (g_all, lax.ppermute(g_all, "dp", [(a, a ^ 2) for a in range(dp)]))
    part = sum([part[0].astype(F32)] + [shift(part[s], "x", -s).astype(F32) for s in range(1, nx)]).astype(BF16)

    block = 1024
    gw_shape = jax.ShapeDtypeStruct((layers, width, d), F32)
    gw_spec = pl.BlockSpec((layers, width, block), lambda n, at: (0, 0, n))
    grad_w = pl.pallas_call(
        weights_kernel,
        grid_spec=pltpu.PrefetchScalarGridSpec(
            num_scalar_prefetch=1,
            grid=(d // block,),
            in_specs=[pl.BlockSpec((2,) + g.shape, lambda n, at: (0, 0, 0))] * 2 + [pl.BlockSpec((full.shape[0], block), lambda n, at: (0, n))],
            out_specs=(gw_spec, gw_spec),
            scratch_shapes=[pltpu.VMEM((dp,) + g.shape, F32), pltpu.VMEM((full.shape[0], cols), F32), pltpu.VMEM((cols, full.shape[0]), BF16)],
        ),
        out_shape=(gw_shape, gw_shape),
        compiler_params=pltpu.CompilerParams(vmem_limit_bytes=56 * 1024 * 1024),
        cost_estimate=cost(2 * cols * full.size, 2 * full.size + 4 * cols * d),
    )(at, *g_all, full)

    qa[2] = shift(qa[2], "dp", -2)
    part, qa[1], qa[3] = lax.optimization_barrier((part, qa[1], qa[3]))
    qa[1], qa[2], qa[3] = lax.optimization_barrier((qa[1], qa[2], qa[3]))
    qa[1], qa[3] = shift(qa[1], "dp", -1), shift(qa[3], "dp", -3)

    part = lax.all_to_all(part.reshape(nz, few, d), "z", 0, 0)
    part, grad_w_key, grad_w_value = lax.optimization_barrier((part, *grad_w))
    part = jnp.sum(part.astype(F32), axis=0).astype(BF16)
    parts = [part] + [shift(part, "dp", s) for s in range(1, dp)]
    parts = jnp.concatenate([parts[-1 - j % dp] for j in range(2 * dp - 1)], axis=0)
    grad_memory = lax.dynamic_slice(parts, ((dp - 1 - here) * few, 0), (mine, d)).astype(F32)
    part, *qa = lax.optimization_barrier((part, *qa))
    qa = sum(a.astype(F32) for a in qa).astype(BF16)
    grad_queries, attended = qa[:, :width].swapaxes(1, 2), qa[:, width:].swapaxes(1, 2)
    return (attended, grad_queries, grad_memory, grad_w_key, grad_w_value)


def solution(mesh):
    dp = mesh.shape["dp"]
    split = Mesh(mesh.devices.reshape(dp, -1, 4, 2), ("dp", "z", "x", "core"))
    mp = ("z", "x", "core")
    by_rows, by_heads = P(None, "dp", mp), P(None, mp, None)
    return jax.shard_map(
        shards,
        mesh=split,
        in_specs=(by_rows, P(mp, None), by_heads, by_heads, by_rows),
        out_specs=(by_rows, by_rows, P(mp, None), by_heads, by_heads),
        check_vma=False,
    )
```

```python
import jax
import jax.numpy as jnp
from jax import lax
from jax.experimental import pallas as pl
from jax.experimental.pallas import tpu as pltpu
from jax.sharding import Mesh
from jax.sharding import PartitionSpec as P

HEAD_WIDTH = 64
BF16 = jnp.bfloat16
F32 = jnp.float32
NT = (((1,), (1,)), ((), ()))


def mm(a, b, dims=(((1,), (0,)), ((), ()))):
    return lax.dot_general(a, b, dims, preferred_element_type=F32)


def shift(x, axis, by):
    n = lax.axis_size(axis)
    return lax.ppermute(x, axis, [(a, (a + by) % n) for a in range(n)])


def after(x, *others):
    return lax.optimization_barrier((x, *others))[0]


def split_heads(own_ref, other_ref, layer):
    lanes = slice(layer * 2 * HEAD_WIDTH, (layer + 1) * 2 * HEAD_WIDTH)
    both = jnp.concatenate([own_ref[:, lanes], other_ref[:, lanes]], axis=0).astype(F32)
    left = lax.broadcasted_iota(jnp.int32, both.shape, 1) < HEAD_WIDTH
    keys = jnp.where(left, both, 0.0).astype(BF16)
    values = jnp.where(left, 0.0, both).astype(BF16)
    return keys, values


def project_kernel(own_key, own_value, other_key, other_value, *refs):
    *mem_refs, own_ref, other_ref = refs
    mem = jnp.concatenate([m[...] for m in mem_refs], axis=0)
    layers, width, _ = own_key.shape
    for key, value, out_ref in ((other_key, other_value, other_ref), (own_key, own_value, own_ref)):
        for layer in range(layers):
            w = jnp.concatenate([key[layer], value[layer]], axis=0)
            at = 2 * layer * width
            out_ref[:, at : at + 2 * width] = mm(w, mem, NT).T.astype(BF16)


def memory_kernel(own_ref, other_ref, own_key, own_value, other_key, other_value, *out_refs):
    layers, width, d = own_key.shape
    blocks, rows = len(out_refs), out_refs[0].shape[0]
    g = jnp.concatenate([own_ref[: blocks * rows], other_ref[...]], axis=1)
    step = 512
    for at in range(0, d, step):
        w = [r[layer, :, at : at + step] for k, v in ((own_key, own_value), (other_key, other_value)) for layer in range(layers) for r in (k, v)]
        out = mm(g, jnp.concatenate(w, axis=0)).astype(BF16)
        for x, out_ref in enumerate(out_refs):
            out_ref[:, at : at + step] = out[x * rows : (x + 1) * rows]


def stats_kernel(own_ref, other_ref, *refs):
    *qdo_refs, stats_ref = refs
    layers, _, rows = qdo_refs[0].shape
    stats_ref[...] = jnp.zeros_like(stats_ref)
    for layer in range(layers):
        keys, values = split_heads(own_ref, other_ref, layer)
        for part, qdo_ref in enumerate(qdo_refs):
            q = qdo_ref[layer]
            scores = mm(keys, q)
            grads = mm(values, q)
            top = jnp.max(scores, axis=0, keepdims=True)
            e = jnp.exp(scores - top)
            total = jnp.sum(e, axis=0, keepdims=True)
            delta = jnp.sum(e * grads, axis=0, keepdims=True) / total
            at = slice(part * rows, (part + 1) * rows)
            stats_ref[layer : layer + 1, at] = top + jnp.log(total)
            stats_ref[layers + layer : layers + layer + 1, at] = delta


def combine(stats_refs, rows, layers):
    parts = len(stats_refs)
    for part in range(parts):
        stats = []
        for k, s in enumerate(stats_refs):
            at = (part - k) % parts * rows
            stats.append(s[:, at : at + rows])
        lses = [s[0:layers] for s in stats]
        top = jnp.maximum(jnp.maximum(lses[0], lses[1]), jnp.maximum(lses[2], lses[3]))
        lse = top + jnp.log(sum(jnp.exp(a - top) for a in lses))
        yield lse, sum(jnp.exp(s[0:layers] - lse) * s[layers : 2 * layers] for s in stats)


def probs_and_scores(keys, values, q, lse, delta):
    probs = jnp.exp(mm(keys, q) - lse)
    dscores = probs * (mm(values, q) - delta)
    return jnp.concatenate([dscores.astype(BF16), probs.astype(BF16)], axis=0)


def grads_kernel(own_ref, other_ref, *refs):
    n = len(refs) // 3
    qdo_refs, stats_refs, g_ref, qa_refs = refs[:n], refs[n : 2 * n], refs[2 * n], refs[2 * n + 1 :]
    layers, width, rows = qdo_refs[0].shape
    tokens = 2 * own_ref.shape[0]
    left = lax.broadcasted_iota(jnp.int32, (tokens, width), 1) < HEAD_WIDTH
    stats = list(combine(stats_refs, rows, layers))
    for layer in range(layers):
        keys, values = split_heads(own_ref, other_ref, layer)
        flipped = jnp.concatenate([keys, values], axis=0).astype(F32).T.astype(BF16)
        acc = 0.0
        for part, (qdo_ref, (lse, delta)) in enumerate(zip(qdo_refs, stats)):
            q = qdo_ref[layer]
            both = probs_and_scores(keys, values, q, lse[layer : layer + 1], delta[layer : layer + 1])
            acc += mm(both, q, NT)
            qa_refs[part][layer] = mm(flipped, both).astype(BF16)
        g_ref[:, layer * width : (layer + 1) * width] = jnp.where(left, acc[:tokens], acc[tokens:]).astype(BF16)


def weights_kernel(at_ref, *refs):
    *g_refs, mem_ref, key_ref, value_ref, stack, order, flipped = refs
    ndp, nx, nz, few = 2 * len(g_refs), 4, 8, 4
    layers, width, _ = key_ref.shape

    @pl.when(pl.program_id(0) == 0)
    def _():
        for pair, g_ref in enumerate(g_refs):
            for part in range(2):
                stack[2 * pair + part] = g_ref[part].astype(F32)
        parts = [lax.bitwise_xor(at_ref[0], dp) for dp in range(ndp)]
        for half in range(2):
            core = at_ref[2] if half == 0 else 1 - at_ref[2]
            for back in range(nx):
                x = lax.rem(at_ref[1] + nx - back, nx)
                first = (half * nx + back) * nz * few
                blocks = [stack[part, first : first + nz * few] for part in parts]
                for z in range(nz):
                    to = pl.multiple_of(((z * nx + x) * 2 + core) * ndp * few, ndp * few)
                    order[pl.ds(to, ndp * few)] = jnp.concatenate([b[z * few : (z + 1) * few] for b in blocks], axis=0)
        flipped[...] = order[...].T.astype(BF16)

    out = mm(flipped[...], mem_ref[...])
    for layer in range(layers):
        at = 2 * layer * width
        key_ref[layer] = out[at : at + width]
        value_ref[layer] = out[at + width : at + 2 * width]


def cost(flops, moved, exps=0):
    return pl.CostEstimate(flops=flops, bytes_accessed=moved, transcendentals=exps)


def shards(queries, memory, w_key, w_value, grad_out):
    layers, rows, width = queries.shape
    dp, nz, nx = lax.axis_size("dp"), lax.axis_size("z"), lax.axis_size("x")
    mine, d = memory.shape
    few = mine // dp
    here = lax.axis_index("dp")
    cols = 2 * width * layers
    half = few * nz * nx
    params = pltpu.CompilerParams(vmem_limit_bytes=28 * 1024 * 1024)

    at = jnp.stack([here, lax.axis_index("x"), lax.axis_index("core")])

    full = lax.all_gather(memory, ("z", "x", "core"), axis=0, tiled=True)

    quarter = lax.dynamic_slice(memory, (here * few, 0), (few, d))
    along_z = lax.all_to_all(jnp.broadcast_to(quarter, (nz, few, d)), "z", 0, 0).reshape(nz * few, d)
    key_other, value_other = shift(w_key, "core", 1), shift(w_value, "core", 1)
    along_z, key_other, value_other, at = lax.optimization_barrier((along_z, key_other, value_other, at))
    qdo = jnp.concatenate([queries.swapaxes(1, 2), grad_out.swapaxes(1, 2)], axis=1)
    qdo = after(qdo, along_z)
    qdo = [qdo] + [shift(qdo, "dp", s) for s in range(1, dp)]

    mem_parts = [along_z] + [shift(along_z, "x", s) for s in range(1, nx)]

    weights = (w_key, w_value, key_other, value_other)
    kv_own, kv_other = pl.pallas_call(
        project_kernel,
        out_shape=(jax.ShapeDtypeStruct((half, cols), BF16), jax.ShapeDtypeStruct((half, cols), BF16)),
        compiler_params=params,
        cost_estimate=cost(4 * half * cols * d, 2 * (half + 2 * cols) * d),
    )(*weights, *mem_parts)
    kv_other = shift(kv_other, "core", 1)

    all_rows = dp * rows
    work = layers * all_rows * 2 * half * 256
    stats = pl.pallas_call(
        stats_kernel,
        out_shape=jax.ShapeDtypeStruct((8, all_rows), F32),
        compiler_params=params,
        cost_estimate=cost(4 * work, 4 * dp * qdo[0].size, layers * all_rows * 2 * half),
    )(kv_own, kv_other, *qdo)
    others = [shift(stats, "dp", s) for s in range(1, dp)]
    g, *qa = pl.pallas_call(
        grads_kernel,
        out_shape=[jax.ShapeDtypeStruct((2 * half, cols), BF16)] + [jax.ShapeDtypeStruct(qdo[0].shape, BF16)] * dp,
        compiler_params=params,
        cost_estimate=cost(12 * work, 8 * dp * qdo[0].size, layers * all_rows * 2 * half),
    )(kv_own, kv_other, *qdo, stats, *others)

    g_other = shift(g[half:], "core", 1)
    part = pl.pallas_call(
        memory_kernel,
        out_shape=[jax.ShapeDtypeStruct((nz * few, d), BF16)] * nx,
        compiler_params=params,
        cost_estimate=cost(4 * half * cols * d, 2 * (half + 2 * cols) * d),
    )(g, g_other, *weights)
    g_all = jnp.stack([g, lax.ppermute(g, "dp", [(a, a ^ 1) for a in range(dp)])])
    g_all = (g_all, lax.ppermute(g_all, "dp", [(a, a ^ 2) for a in range(dp)]))
    part = sum([part[0].astype(F32)] + [shift(part[s], "x", -s).astype(F32) for s in range(1, nx)]).astype(BF16)

    block = 2048
    gw_shape = jax.ShapeDtypeStruct((layers, width, d), F32)
    gw_spec = pl.BlockSpec((layers, width, block), lambda n, at: (0, 0, n))
    grad_w = pl.pallas_call(
        weights_kernel,
        grid_spec=pltpu.PrefetchScalarGridSpec(
            num_scalar_prefetch=1,
            grid=(d // block,),
            in_specs=[pl.BlockSpec((2,) + g.shape, lambda n, at: (0, 0, 0))] * 2 + [pl.BlockSpec((full.shape[0], block), lambda n, at: (0, n))],
            out_specs=(gw_spec, gw_spec),
            scratch_shapes=[pltpu.VMEM((dp,) + g.shape, F32), pltpu.VMEM((full.shape[0], cols), F32), pltpu.VMEM((cols, full.shape[0]), BF16)],
        ),
        out_shape=(gw_shape, gw_shape),
        compiler_params=pltpu.CompilerParams(vmem_limit_bytes=56 * 1024 * 1024),
        cost_estimate=cost(2 * cols * full.size, 2 * full.size + 4 * cols * d),
    )(at, *g_all, full)

    qa[2] = shift(qa[2], "dp", -2)
    part, qa[1], qa[3] = lax.optimization_barrier((part, qa[1], qa[3]))
    qa[1], qa[2], qa[3] = lax.optimization_barrier((qa[1], qa[2], qa[3]))
    qa[1], qa[3] = shift(qa[1], "dp", -1), shift(qa[3], "dp", -3)

    part = lax.all_to_all(part.reshape(nz, few, d), "z", 0, 0)
    part, grad_w_key, grad_w_value = lax.optimization_barrier((part, *grad_w))
    part = jnp.sum(part.astype(F32), axis=0).astype(BF16)
    parts = [part] + [shift(part, "dp", s) for s in range(1, dp)]
    parts = jnp.concatenate([parts[-1 - j % dp] for j in range(2 * dp - 1)], axis=0)
    grad_memory = lax.dynamic_slice(parts, ((dp - 1 - here) * few, 0), (mine, d)).astype(F32)
    part, *qa = lax.optimization_barrier((part, *qa))
    qa = sum(a.astype(F32) for a in qa).astype(BF16)
    grad_queries, attended = qa[:, :width].swapaxes(1, 2), qa[:, width:].swapaxes(1, 2)
    return (attended, grad_queries, grad_memory, grad_w_key, grad_w_value)


def solution(mesh):
    dp = mesh.shape["dp"]
    split = Mesh(mesh.devices.reshape(dp, -1, 4, 2), ("dp", "z", "x", "core"))
    mp = ("z", "x", "core")
    by_rows, by_heads = P(None, "dp", mp), P(None, mp, None)
    return jax.shard_map(
        shards,
        mesh=split,
        in_specs=(by_rows, P(mp, None), by_heads, by_heads, by_rows),
        out_specs=(by_rows, by_rows, P(mp, None), by_heads, by_heads),
        check_vma=False,
    )
```
